256 devices in a mesh: slab: 256 (over x, z, y, core).
Axes of the slice: x: 4, y: 4, z: 8, core: 2. Of those that a mesh axis runs over, the one named last changes fastest.
Arguments:
- velocity: bfloat16 [3, 1024, 16, 4096], P(None, 'slab'), may hold values from -6 to 6
Outputs:
- composite: float32 [4, 32768], P(None, 'slab')
The draws below stay inside these ranges and needn't reach their ends.
All inputs are finite; a program needn't handle non-finite values.
Results may differ from the reference program's by a relative error of at most 0.00085.
Values may be sent and summed in bfloat16 or wider, within the bound.
No kernel may reach another device: no remote copies, remote signals or barrier semaphores. Data moves between devices by JAX's collectives and lax.ppermute only.
A program may use at most 192 MiB of HBM per device.

```python
import jax
import jax.numpy as jnp
from jax import lax

CZ = 4
BAND = 8
NX = 4096
YH = 16
NZ = 1024
N_SLAB = 256


def steps_of(rng, dims, split, low, high):
    loudness, own = 1.0, jax.random.fold_in(rng, 6)
    for dim, shards_of in split:
        heights = jnp.exp(jax.random.uniform(jax.random.fold_in(own, dim), (shards_of,), jnp.float32, low / len(split), high / len(split)))
        loudness = loudness * jnp.repeat(heights, dims[dim] // shards_of).reshape([-1 if axis == dim else 1 for axis in range(len(dims))])
    return loudness


def bell_draw(key, extent, deviation, most, cuts=(), kind=jnp.bfloat16):
    level = steps_of(key, extent, cuts, -0.22, 0.18) if cuts else 1.0
    result = jax.random.normal(key, extent, jnp.float32) * deviation * level
    return jnp.minimum(jnp.maximum(result, -most), most).astype(kind)


def setup_inputs(seed: int = 0) -> dict:
    key_of = jax.random.split(jax.random.key(seed), 2)
    velocity = bell_draw(key_of[0], (3, NZ, YH, NX), 1.0, 6.0, ((1, 256),))
    return {"velocity": velocity}


taps = (1.0 / 16.0, 4.0 / 16.0, 6.0 / 16.0, 4.0 / 16.0, 1.0 / 16.0)
opacity_gain = 5.0
colour_gain = 2.0


def smooth_valid(field, along):
    length = field.shape[along]
    total = taps[0] * lax.slice_in_dim(field, 0, length - 4, axis=along)
    for offset in range(1, 5):
        total = total + taps[offset] * lax.slice_in_dim(field, offset, length - 4 + offset, axis=along)
    return total


def smooth_wrap(field, along):
    total = taps[0] * jnp.roll(field, 2, along)
    for offset in range(1, 5):
        total = total + taps[offset] * jnp.roll(field, 2 - offset, along)
    return total


def derive_valid(field, along):
    length = field.shape[along]
    first = lax.slice_in_dim(field, 0, length - 4, axis=along)
    second = lax.slice_in_dim(field, 1, length - 3, axis=along)
    fourth = lax.slice_in_dim(field, 3, length - 1, axis=along)
    fifth = lax.slice_in_dim(field, 4, length, axis=along)
    return (first - 8.0 * second + 8.0 * fourth - fifth) / 12.0


def derive_wrap(field, along):
    return (jnp.roll(field, 2, along) - 8.0 * jnp.roll(field, 1, along) + 8.0 * jnp.roll(field, -1, along) - jnp.roll(field, -2, along)) / 12.0


def slab_image(smoothed, planes_total):
    comp_x = smoothed[0]
    comp_y = smoothed[1]
    comp_z = smoothed[2]

    def along_z(field):
        return derive_valid(field, 0)[:, 2:-2]

    def along_y(field):
        return derive_valid(field[2:-2], 1)

    def along_x(field):
        return derive_wrap(field[2:-2, 2:-2], 2)

    curl_x = along_y(comp_z) - along_z(comp_y)
    curl_y = along_z(comp_x) - along_x(comp_z)
    curl_z = along_x(comp_y) - along_y(comp_x)
    density = opacity_gain * (curl_x * curl_x + curl_y * curl_y + curl_z * curl_z) / planes_total
    colour = jax.nn.sigmoid(colour_gain * smoothed[:, 2:-2, 2:-2])
    running = jnp.cumsum(density, axis=0)
    before = jnp.concatenate([jnp.zeros_like(density[:1]), running[:-1]], axis=0)
    weight = jnp.exp(-before) * (1.0 - jnp.exp(-density))
    colour_sum = jnp.sum(weight[None] * colour, axis=1)
    colour_sum = colour_sum.reshape(3, -1)
    depth = jnp.sum(density, axis=0).reshape(-1)
    return colour_sum, depth


def reference(velocity):
    def step(carry, block):
        colour_acc, depth_acc = carry
        start = block * CZ
        planes = (start - 4 + jnp.arange(CZ + 8, dtype=jnp.int32)) % NZ
        piece = jnp.take(velocity, planes.astype(jnp.int32), axis=1).astype(jnp.float32)
        smoothed = smooth_wrap(smooth_valid(smooth_valid(piece, 1), 2), 3)
        colour_part, depth_part = slab_image(smoothed, NZ)
        colour_acc = colour_acc + jnp.exp(-depth_acc)[None] * colour_part
        depth_acc = depth_acc + depth_part
        return (colour_acc, depth_acc), None

    start_colour = jnp.zeros((3, BAND * NX), jnp.float32)
    start_depth = jnp.zeros((BAND * NX,), jnp.float32)
    (colour_acc, depth_acc), unused = lax.scan(step, (start_colour, start_depth), jnp.arange(N_SLAB, dtype=jnp.int32))
    return jnp.concatenate([colour_acc, (1.0 - jnp.exp(-depth_acc))[None]], axis=0)
```

```python
import numpy as np
import jax
import jax.numpy as jnp
from jax import lax
from jax.experimental import pallas as pl
from jax.experimental.pallas import tpu as pltpu
from jax.sharding import PartitionSpec as P

NX = 4096
TILES = NX // 128
S_INT = {-2: 1, -1: 4, 0: 6, 1: 4, 2: 1}
D_INT = {-2: 1, -1: -8, 1: 8, 2: -1}
DS_INT = {}
for i, a in S_INT.items():
    for j, b in D_INT.items():
        DS_INT[i + j] = DS_INT.get(i + j, 0) + a * b
UX, UY, UZ = 0, 1, 2
OPACITY_GAIN = 5.0


def own_row(c, z, y):
    return (c * 4 + z) * 16 + y


PARTS = ((UX, True, 12), (UZ, True, 12), (UY, True, 8), (UX, False, 8), (UY, False, 8))


def message_rows():
    rows = []
    for c, inner, count in PARTS:
        for k in range(2):
            for i in range(count):
                rows.append((c, inner, k, i + (2 if count == 12 else 4)))
    return rows


def message_plane(inner, k, up):
    return (2 + k if inner else k) if up else (k if inner else 2 + k)


def send_matrix(up):
    w = np.zeros((96, 192), np.float32)
    for n, (c, inner, k, y) in enumerate(message_rows()):
        for dy, t in S_INT.items():
            w[n, own_row(c, message_plane(inner, k, up), y + dy)] += t
    return w


TERMS = (
    (0, UX, "S", "S", 1),
    (1, UY, "S", "S", 1),
    (2, UZ, "S", "S", 1),
    (3, UZ, "S", "D", 1),
    (3, UY, "D", "S", -1),
    (4, UX, "D", "S", 1),
    (5, UX, "S", "D", -1),
)


def field_matrices():
    own = np.zeros((192, 192), np.float32)
    halo = {False: np.zeros((192, 96), np.float32), True: np.zeros((192, 96), np.float32)}
    place = {up: {} for up in (False, True)}
    for up in (False, True):
        for n, (c, inner, k, y) in enumerate(message_rows()):
            plane = message_plane(inner, k, up) + (-4 if up else 4)
            place[up][c, plane, y] = n
    along = {"S": S_INT, "D": DS_INT}
    for field, c, fz, fy, sign in TERMS:
        for p in range(4):
            for r in range(8):
                m = field * 32 + p * 8 + r
                for dz, a in along[fz].items():
                    q = p + dz
                    if 0 <= q < 4:
                        for dy, b in along[fy].items():
                            own[m, own_row(c, q, r + 4 + dy)] += sign * a * b
                    else:
                        up = q < 0
                        if fy == "S":
                            halo[up][m, place[up][c, q, r + 4]] += sign * a
                        else:
                            for dy, b in D_INT.items():
                                halo[up][m, place[up][c, q, r + 4 + dy]] += sign * a * b
    return own, halo[True], halo[False]


def matrices():
    up, down = send_matrix(True), send_matrix(False)
    send = np.stack([np.concatenate([down, up]), np.concatenate([up, down])])
    own, prev, nxt = field_matrices()
    field = np.stack([np.concatenate([own, prev, nxt], 1), np.concatenate([own, nxt, prev], 1)])
    return send.astype(jnp.bfloat16), field.astype(jnp.bfloat16)


def core_index():
    return lax.rem(lax.axis_index("slab"), 2)


def pack_kernel(w_ref, x_ref, a_ref, b_ref):
    w = w_ref[core_index()]
    out = jnp.dot(w, x_ref[...], preferred_element_type=jnp.float32).astype(jnp.bfloat16)
    a_ref[...] = out[:96]
    b_ref[...] = out[96:]


def pack(w, x):
    chunk = 1024
    return pl.pallas_call(
        pack_kernel,
        grid=(NX // chunk,),
        out_shape=[jax.ShapeDtypeStruct((96, NX), jnp.bfloat16)] * 2,
        in_specs=[
            pl.BlockSpec((2, 192, 192), lambda i: (0, 0, 0)),
            pl.BlockSpec((192, chunk), lambda i: (0, i)),
        ],
        out_specs=[pl.BlockSpec((96, chunk), lambda i: (0, i))] * 2,
        compiler_params=pltpu.CompilerParams(vmem_limit_bytes=32 << 20),
        name="pack_halo",
    )(w, x)


def slab_kernel(w_ref, x_ref, a_ref, b_ref, keep_ref, send_ref, field_ref):
    core = core_index()
    w = w_ref[core]
    chunk = 512

    def multiply(n, carry):
        cols = pl.ds(pl.multiple_of(n * chunk, chunk), chunk)
        rows = jnp.concatenate([x_ref[:, cols], a_ref[:, cols], b_ref[:, cols]], axis=0)
        field_ref[:, cols] = jnp.dot(w, rows, preferred_element_type=jnp.float32)
        return carry

    lax.fori_loop(0, NX // chunk, multiply, 0)
    lane = lax.broadcasted_iota(jnp.int32, (32, 128), 1)

    def tile(t, out_ref, row):
        def cols(k):
            return pl.ds(pl.multiple_of(lax.rem(t + k + TILES, TILES) * 128, 128), 128)

        at = [cols(-1), cols(0), cols(1)]

        def load(field):
            return [field_ref[field * 32 : field * 32 + 32, at[k]] for k in range(3)]

        def ahead(v, i):
            return pltpu.roll(jnp.where(lane < i, v[2], v[1]), 128 - i, 1)

        def behind(v, i):
            return pltpu.roll(jnp.where(lane >= 128 - i, v[0], v[1]), i, 1)

        def smooth(v, a1, b1, a2, b2):
            return 6.0 * v[1] + 4.0 * (a1 + b1) + (a2 + b2)

        def smoothed(field):
            v = load(field)
            return smooth(v, ahead(v, 1), behind(v, 1), ahead(v, 2), behind(v, 2))

        def smoothed_and_derivative(field):
            v = load(field)
            ups = [ahead(v, i) for i in range(1, 5)]
            downs = [behind(v, i) for i in range(1, 5)]
            difference = [u - d for u, d in zip(ups, downs)]
            derivative = 36.0 * difference[0] + 26.0 * difference[1] + (4.0 * difference[2] - difference[3])
            return smooth(v, ups[0], downs[0], ups[1], downs[1]), derivative

        s_x = smoothed(0)
        s_y, dx_y = smoothed_and_derivative(1)
        s_z, dx_z = smoothed_and_derivative(2)
        curl_x = smoothed(3)
        curl_y = smoothed(4) - dx_z
        curl_z = smoothed(5) + dx_y
        density = (curl_x * curl_x + curl_y * curl_y + curl_z * curl_z) * (OPACITY_GAIN / 1024.0 / 49152.0**2)
        colours = [0.5 + 0.5 * jnp.tanh(s * (1.0 / 4096.0)) for s in (s_x, s_y, s_z)]
        opacity = 1.0 - jnp.exp(-density)
        depth = density[:8]
        weight = opacity[:8]
        sums = [weight * c[:8] for c in colours]
        for p in range(1, 4):
            part = slice(8 * p, 8 * p + 8)
            weight = jnp.exp(-depth) * opacity[part]
            sums = [s + weight * c[part] for s, c in zip(sums, colours)]
            depth = depth + density[part]
        for f, value in enumerate(sums + [depth]):
            out_ref[pl.ds(row * 4 + f, 8, stride=64), :] = value

    def pair(i, carry):
        tile(2 * i + core, keep_ref, i)
        tile(2 * i + 1 - core, send_ref, i)
        return carry

    lax.fori_loop(0, TILES // 2, pair, 0)


def slab_image(w, x, a, b):
    vmem = pl.BlockSpec(memory_space=pltpu.VMEM)
    return pl.pallas_call(
        slab_kernel,
        out_shape=[jax.ShapeDtypeStruct((512, 128), jnp.float32)] * 2,
        in_specs=[vmem] * 4,
        out_specs=[vmem] * 2,
        scratch_shapes=[pltpu.VMEM((192, NX), jnp.float32)],
        compiler_params=pltpu.CompilerParams(vmem_limit_bytes=32 << 20),
        name="slab_image",
    )(w, x, a, b)


def merge_kernel(own_ref, other_ref, out_ref):
    first = core_index() == 0

    def rows(f):
        return pl.ds(f, 128, stride=4)

    own_depth, other_depth = own_ref[rows(3), :], other_ref[rows(3), :]
    zero = jnp.zeros_like(own_depth)
    own_scale = jnp.exp(-jnp.where(first, zero, other_depth))
    other_scale = jnp.exp(-jnp.where(first, own_depth, zero))
    for f in range(3):
        out_ref[rows(f), :] = own_scale * own_ref[rows(f), :] + other_scale * other_ref[rows(f), :]
    out_ref[rows(3), :] = own_depth + other_depth


def merge(own, other):
    vmem = pl.BlockSpec(memory_space=pltpu.VMEM)
    return pl.pallas_call(
        merge_kernel,
        out_shape=jax.ShapeDtypeStruct((512, 128), jnp.float32),
        in_specs=[vmem] * 2,
        out_specs=vmem,
        compiler_params=pltpu.CompilerParams(vmem_limit_bytes=8 << 20),
        name="merge_cores",
    )(own, other)


def composite_kernel(in_ref, out_ref):
    def part(v, f):
        return in_ref[pl.ds(v * 4 + f, 8, stride=64), :]

    depth = part(0, 3)
    sums = [part(0, f) for f in range(3)]
    for v in range(1, 16):
        through = jnp.exp(-depth)
        sums = [s + through * part(v, f) for f, s in enumerate(sums)]
        depth = depth + part(v, 3)
    nearer = [jnp.zeros((1, 128), jnp.float32)]
    for s in range(8):
        nearer.append(nearer[-1] + depth[s : s + 1])
    through = jnp.exp(-jnp.concatenate(nearer[:8], axis=0))
    for f in range(3):
        out_ref[f : f + 1, :] = jnp.sum(through * sums[f], axis=0, keepdims=True)
    out_ref[3:4, :] = 1.0 - jnp.exp(-nearer[8])


def composite(parts):
    vmem = pl.BlockSpec(memory_space=pltpu.VMEM)
    return pl.pallas_call(
        composite_kernel,
        out_shape=jax.ShapeDtypeStruct((4, 128), jnp.float32),
        in_specs=[vmem],
        out_specs=vmem,
        compiler_params=pltpu.CompilerParams(vmem_limit_bytes=8 << 20),
        name="composite_chips",
    )(parts)


def solution(mesh):
    devices = mesh.shape["slab"]
    send_weights, field_weights = matrices()
    across = [(i, (i + 1) % devices if i % 2 else (i - 1) % devices) for i in range(devices)]
    within = [(i, i ^ 1) for i in range(devices)]
    same_core = [list(range(k, devices, 2)) for k in range(2)]

    def per_device(velocity):
        x = velocity.reshape(192, NX)
        to_chip, to_core = pack(jnp.asarray(send_weights), x)
        from_chip = lax.ppermute(to_chip, "slab", across)
        from_core = lax.ppermute(to_core, "slab", within)
        keep, send = slab_image(jnp.asarray(field_weights), x, from_chip, from_core)
        other = lax.ppermute(send, "slab", within)
        merged = merge(keep, other).reshape(128, 4, 128)
        gathered = lax.all_to_all(merged, "slab", 0, 0, axis_index_groups=same_core, tiled=True)
        return composite(gathered.reshape(512, 128))

    return jax.shard_map(per_device, mesh=mesh, in_specs=(P(None, "slab", None, None),), out_specs=P(None, "slab"), check_vma=False)
```

```python
import functools

import numpy as np
import jax
import jax.numpy as jnp
from jax import lax
from jax.experimental import pallas as pl
from jax.experimental.pallas import tpu as pltpu
from jax.sharding import PartitionSpec as P

NX = 4096
TILES = NX // 128
S_INT = {-2: 1, -1: 4, 0: 6, 1: 4, 2: 1}
D_INT = {-2: 1, -1: -8, 1: 8, 2: -1}
DS_INT = {}
for i, a in S_INT.items():
    for j, b in D_INT.items():
        DS_INT[i + j] = DS_INT.get(i + j, 0) + a * b
UX, UY, UZ = 0, 1, 2
OPACITY_GAIN = 5.0


def own_row(c, z, y):
    return (c * 4 + z) * 16 + y


PARTS = ((UX, True, 12), (UX, False, 8), (UY, True, 8), (UY, False, 8), (UZ, True, 12))


def message_rows():
    rows = []
    for c, inner, count in PARTS:
        for k in range(2):
            for i in range(count):
                rows.append((c, inner, k, i + (2 if count == 12 else 4)))
    return rows


def message_plane(inner, k, up):
    return (2 + k if inner else k) if up else (k if inner else 2 + k)


def send_matrix(up):
    w = np.zeros((96, 192), np.float32)
    for n, (c, inner, k, y) in enumerate(message_rows()):
        for dy, t in S_INT.items():
            w[n, own_row(c, message_plane(inner, k, up), y + dy)] += t
    return w


TERMS = (
    (0, UY, "S", "S", 1),
    (1, UZ, "S", "S", 1),
    (2, UZ, "S", "D", 1),
    (2, UY, "D", "S", -1),
    (3, UX, "S", "S", 1),
    (4, UX, "D", "S", 1),
    (5, UX, "S", "D", -1),
)
OWN_YZ, OWN_X, HALO_YZ, HALO_X = slice(64, 192), slice(0, 64), slice(32, 96), slice(0, 48)


def field_matrices():
    own = np.zeros((192, 192), np.float32)
    halo = {False: np.zeros((192, 96), np.float32), True: np.zeros((192, 96), np.float32)}
    place = {up: {} for up in (False, True)}
    for up in (False, True):
        for n, (c, inner, k, y) in enumerate(message_rows()):
            plane = message_plane(inner, k, up) + (-4 if up else 4)
            place[up][c, plane, y] = n
    along = {"S": S_INT, "D": DS_INT}
    for field, c, fz, fy, sign in TERMS:
        for p in range(4):
            for r in range(8):
                m = field * 32 + p * 8 + r
                for dz, a in along[fz].items():
                    q = p + dz
                    if 0 <= q < 4:
                        for dy, b in along[fy].items():
                            own[m, own_row(c, q, r + 4 + dy)] += sign * a * b
                    else:
                        up = q < 0
                        if fy == "S":
                            halo[up][m, place[up][c, q, r + 4]] += sign * a
                        else:
                            for dy, b in D_INT.items():
                                halo[up][m, place[up][c, q, r + 4 + dy]] += sign * a * b
    return own, halo[True], halo[False]


def line_matrix():
    w = np.zeros((256, 256), np.float32)
    for column, taps in ((0, S_INT), (128, DS_INT)):
        for j in range(128):
            for d, t in taps.items():
                row = j + d if 0 <= j + d < 128 else 128 + (j + d) % 128
                w[row, column + j] += t
    return w


def matrices():
    up, down = send_matrix(True), send_matrix(False)
    send = np.stack([np.concatenate([down, up]), np.concatenate([up, down])])
    own, prev, nxt = field_matrices()
    field = np.zeros((2, 192, 256), np.float32)
    for core, halo in enumerate(([prev, nxt], [nxt, prev])):
        field[core, :96] = np.concatenate([own[:96, OWN_YZ], *(h[:96, HALO_YZ] for h in halo)], 1)
        field[core, 96:, :160] = np.concatenate([own[96:, OWN_X], *(h[96:, HALO_X] for h in halo)], 1)
        assert not own[:96, OWN_X].any() and not own[96:, OWN_YZ].any()
        assert not any(h[:96, :32].any() or h[96:, 48:].any() for h in halo)
    return [m.astype(jnp.bfloat16) for m in (send, field, line_matrix())]


SEGMENTS = ((tuple(range(32)), tuple(range(32))),)
TURN = 123
GROUP = 8
HBM = pl.BlockSpec(memory_space=pltpu.HBM)
VMEM = pl.BlockSpec(memory_space=pltpu.VMEM)


def in_hbm(x):
    return pltpu.with_memory_space_constraint(jnp.asarray(x), pltpu.HBM)


def core_index():
    return lax.rem(lax.axis_index("slab"), 2)


def runs(tiles):
    out = []
    for place, tile in enumerate(tiles):
        tile %= TILES
        if out and out[-1][0] + out[-1][2] == tile:
            out[-1][2] += 1
        else:
            out.append([tile, place, 1])
    return out


def pack_kernel(segments, w_ref, f_ref, l_ref, x_ref, *refs):
    count = len(segments)
    packed, (fv_ref, lv_ref) = [refs[3 * n : 3 * n + 3] for n in range(count)], refs[3 * count : 3 * count + 2]
    wv_ref, sems = refs[3 * count + 2 :]
    core = core_index()
    first = pltpu.make_async_copy(w_ref.at[core], wv_ref, sems.at[0])
    first.start()
    parts = []
    for tiles, (a_ref, b_ref, xv_ref) in zip(segments, packed):
        for tile, place, length in runs(tiles):
            for k in range(0, length, 16):
                n = min(16, length - k)
                cols = slice((place + k) * 128, (place + k + n) * 128)
                source = x_ref.at[:, pl.ds((tile + k) * 128, n * 128)]
                copy = pltpu.make_async_copy(source, xv_ref.at[:, cols], sems.at[len(parts) + 1])
                copy.start()
                parts.append((copy, a_ref, b_ref, xv_ref, cols))
    later = [
        pltpu.make_async_copy(f_ref.at[core], fv_ref, sems.at[len(parts) + 1]),
        pltpu.make_async_copy(l_ref, lv_ref, sems.at[len(parts) + 2]),
    ]
    for copy in later:
        copy.start()
    first.wait()
    for copy, a_ref, b_ref, xv_ref, cols in parts:
        copy.wait()
        out = jnp.dot(wv_ref[...], xv_ref[:, cols], preferred_element_type=jnp.float32).astype(jnp.bfloat16)
        a_ref[:, cols] = out[:96]
        b_ref[:, cols] = out[96:]
    for copy in later:
        copy.wait()


def pack(segments, w, field_w, line_w, x):
    out = []
    for tiles in segments:
        width = len(tiles) * 128
        out += [(96, width), (96, width), (192, width)]
    out += [(192, 256), (256, 256)]
    *packed, field_w, line_w = pl.pallas_call(
        functools.partial(pack_kernel, segments),
        out_shape=[jax.ShapeDtypeStruct(shape, jnp.bfloat16) for shape in out],
        in_specs=[HBM] * 4,
        out_specs=[VMEM] * len(out),
        scratch_shapes=[pltpu.VMEM((192, 192), jnp.bfloat16), pltpu.SemaphoreType.DMA((24,))],
        compiler_params=pltpu.CompilerParams(vmem_limit_bytes=16 << 20),
        name="pack_halo",
    )(w, field_w, line_w, x)
    return [packed[n : n + 3] for n in range(0, len(packed), 3)], field_w, line_w


def slab_kernel(tiles, image, before, after, *refs):
    w_ref, l_ref, x_ref, a_ref, b_ref = refs[:5]
    edges = dict(zip(before, refs[5:]))
    keep_ref, send_ref, *out_edges = refs[5 + len(before) :]
    core = core_index()
    half = lax.broadcasted_iota(jnp.int32, (192, 128), 1) < 64
    place = {tile % TILES: n for n, tile in enumerate(tiles)}
    fields = {}

    def field(t):
        t %= TILES
        if t in edges:
            return edges[t][:192, :], edges[t][192:, :]
        if t not in fields:
            n = place[t] // 2 * 2
            cols = slice(n * 128, min(n + 2, len(tiles)) * 128)
            yz = jnp.concatenate([x_ref[OWN_YZ, cols], a_ref[HALO_YZ, cols], b_ref[HALO_YZ, cols]], axis=0)
            x = jnp.concatenate([x_ref[OWN_X, cols], a_ref[HALO_X, cols], b_ref[HALO_X, cols]], axis=0)
            out = jnp.concatenate(
                [
                    jnp.dot(w_ref[:96, :], yz, preferred_element_type=jnp.float32),
                    jnp.dot(w_ref[96:, :160], x, preferred_element_type=jnp.float32),
                ],
                axis=0,
            )
            high = out.astype(jnp.bfloat16)
            low = (out - high.astype(jnp.float32)).astype(jnp.bfloat16)
            for k, tile in enumerate(tiles[n : n + 2]):
                part = slice(k * 128, k * 128 + 128)
                tile %= TILES
                fields[tile] = high[:, part], low[:, part]
                if tile in after:
                    ref = out_edges[after.index(tile)]
                    ref[:192, :], ref[192:, :] = fields[tile]
        return fields[t]

    def line(t):
        out = []
        for previous, here, following in zip(field(t - 1), field(t), field(t + 1)):
            out += [here, jnp.where(half, following, previous)]
        return jnp.concatenate(out, axis=1)

    def tile_group(group):
        lines = [line(t) for t in group]
        both = jnp.concatenate([l_ref[...]] * 2, axis=0)
        yz = jnp.dot(jnp.concatenate([v[:64] for v in lines], axis=0), both, preferred_element_type=jnp.float32)
        rest = jnp.dot(jnp.concatenate([v[64:] for v in lines], axis=0), both[:, :128], preferred_element_type=jnp.float32)
        return [tile(yz[n * 64 : n * 64 + 64], rest[n * 128 : n * 128 + 128]) for n in range(len(group))]

    def tile(yz, rest):
        smoothed = [rest[32:64], yz[:32, :128], yz[32:, :128]]
        curl = [rest[:32], rest[64:96] - yz[32:, 128:], rest[96:] + yz[:32, 128:]]
        density = (curl[0] * curl[0] + curl[1] * curl[1] + curl[2] * curl[2]) * (OPACITY_GAIN / 1024.0 / 49152.0**2)
        colours = [0.5 + 0.5 * jnp.tanh(s * (1.0 / 4096.0)) for s in smoothed]
        opacity = 1.0 - jnp.exp(-density)
        depth = density[:8]
        weight = opacity[:8]
        sums = [weight * c[:8] for c in colours]
        for p in range(1, 4):
            part = slice(8 * p, 8 * p + 8)
            weight = jnp.exp(-depth) * opacity[part]
            sums = [s + weight * c[part] for s, c in zip(sums, colours)]
            depth = depth + density[part]
        return sums + [depth]

    pairs = len(image) // 2
    for first in range(0, len(image), GROUP):
        values = tile_group(image[first : first + GROUP])
        for n in range(0, len(values), 2):
            for f, (a, b) in enumerate(zip(values[n], values[n + 1])):
                row = (f * pairs + (first + n) // 2) * 8
                keep_ref[row : row + 8, :] = jnp.where(core == 0, a, b)
                send_ref[row : row + 8, :] = jnp.where(core == 0, b, a)


def slab_image(tiles, image, before, after, *arrays):
    pairs = len(image) // 2
    out = [jax.ShapeDtypeStruct((pairs * 32, 128), jnp.float32)] * 2 + [jax.ShapeDtypeStruct((384, 128), jnp.bfloat16)] * len(after)
    return pl.pallas_call(
        functools.partial(slab_kernel, tiles, image, before, after),
        out_shape=out,
        in_specs=[VMEM] * len(arrays),
        out_specs=[VMEM] * len(out),
        compiler_params=pltpu.CompilerParams(vmem_limit_bytes=16 << 20),
        cost_estimate=pl.CostEstimate(flops=2 * 192 * 1024 * 128 * len(tiles), bytes_accessed=1 << 20, transcendentals=0),
        name="slab_image",
    )(*arrays)


def merge_kernel(images, *refs):
    first = core_index() == 0
    out_ref = refs[-1]
    for image, own_ref, other_ref in zip(images, refs[0:-1:2], refs[1:-1:2]):
        pairs = len(image) // 2
        own, other = ([ref[f * pairs * 8 : (f + 1) * pairs * 8, :] for f in range(4)] for ref in (own_ref, other_ref))
        zero = jnp.zeros_like(own[3])
        own_scale = jnp.exp(-jnp.where(first, zero, other[3]))
        other_scale = jnp.exp(-jnp.where(first, own[3], zero))
        merged = [own_scale * a + other_scale * b for a, b in zip(own[:3], other[:3])] + [own[3] + other[3]]
        for f in range(4):
            for n in range(pairs):
                rank = ((image[0] // 2 + n) % (TILES // 2) - TURN) % 128
                value, turn = merged[f][n * 8 : n * 8 + 8], rank // 16
                out_ref[pl.ds(rank % 16 * 4 + f, 8, stride=64), :] = pltpu.roll(value, turn, 0) if turn else value


def merge(images, arrays):
    return pl.pallas_call(
        functools.partial(merge_kernel, images),
        out_shape=jax.ShapeDtypeStruct((512, 128), jnp.float32),
        in_specs=[VMEM] * len(arrays),
        out_specs=VMEM,
        compiler_params=pltpu.CompilerParams(vmem_limit_bytes=8 << 20),
        name="merge_cores",
    )(*arrays)


def composite_kernel(in_ref, out_ref):
    lead = (-TURN) % 128 // 16

    def part(v, f):
        rank = (v - TURN) % 128
        value = in_ref[pl.ds(rank % 16 * 4 + f, 8, stride=64), :]
        turn = (lead - rank // 16) % 8
        return pltpu.roll(value, turn, 0) if turn else value

    depth = part(0, 3)
    sums = [part(0, f) for f in range(3)]
    for v in range(1, 16):
        through = jnp.exp(-depth)
        sums = [s + through * part(v, f) for f, s in enumerate(sums)]
        depth = depth + part(v, 3)
    nearer, total = {}, jnp.zeros((1, 128), jnp.float32)
    for segment in range(8):
        sublane = (segment + lead) % 8
        nearer[sublane] = total
        total = total + depth[sublane : sublane + 1]
    through = jnp.exp(-jnp.concatenate([nearer[s] for s in range(8)], axis=0))
    for f in range(3):
        out_ref[f : f + 1, :] = jnp.sum(through * sums[f], axis=0, keepdims=True)
    out_ref[3:4, :] = 1.0 - jnp.exp(-total)


def composite(parts):
    return pl.pallas_call(
        composite_kernel,
        out_shape=jax.ShapeDtypeStruct((4, 128), jnp.float32),
        in_specs=[VMEM],
        out_specs=VMEM,
        compiler_params=pltpu.CompilerParams(vmem_limit_bytes=8 << 20),
        name="composite_chips",
    )(parts)


def solution(mesh):
    devices = mesh.shape["slab"]
    weights = matrices()
    across = [(i, (i + 1) % devices if i % 2 else (i - 1) % devices) for i in range(devices)]
    within = [(i, i ^ 1) for i in range(devices)]
    same_core = [[(2 * (c + TURN) + k) % devices for c in range(devices // 2)] for k in range(2)]

    def edges_of():
        takes, owner = [], {}
        for n, (tiles, image) in enumerate(SEGMENTS):
            owner.update({t % TILES: n for t in tiles})
            need = range(image[0] - 1, image[-1] + 2)
            takes.append(sorted({t % TILES for t in need if owner[t % TILES] != n}))
        hands = [sorted({t for take in takes for t in take if owner[t] == n}) for n in range(len(SEGMENTS))]
        return takes, hands

    takes, hands = edges_of()

    def per_device(velocity):
        x = in_hbm(velocity.reshape(192, NX))
        packed, field_w, line_w = pack([tiles for tiles, _ in SEGMENTS], *map(in_hbm, weights), x)
        from_chip = [lax.ppermute(a, "slab", across) for a, _, _ in packed]
        from_core = [lax.ppermute(b, "slab", within) for _, b, _ in packed]
        edges, swapped = {}, []
        for n, (tiles, image) in enumerate(SEGMENTS):
            keep, send, *handed = slab_image(
                tiles, image, takes[n], hands[n], field_w, line_w, packed[n][2], from_chip[n], from_core[n], *(edges[t] for t in takes[n])
            )
            edges.update(zip(hands[n], handed))
            swapped += [keep, lax.ppermute(send, "slab", within)]
        merged = merge([image for _, image in SEGMENTS], swapped).reshape(128, 4, 128)
        gathered = lax.all_to_all(merged, "slab", 0, 0, axis_index_groups=same_core, tiled=True)
        return composite(gathered.reshape(512, 128))

    return jax.shard_map(per_device, mesh=mesh, in_specs=(P(None, "slab", None, None),), out_specs=P(None, "slab"), check_vma=False)
```

```python
import numpy as np
import jax
import jax.numpy as jnp
from jax import lax
from jax.experimental import pallas as pl
from jax.experimental.pallas import tpu as pltpu
from jax.sharding import PartitionSpec as P

NX = 4096
TILES = NX // 128
S_INT = {-2: 1, -1: 4, 0: 6, 1: 4, 2: 1}
D_INT = {-2: 1, -1: -8, 1: 8, 2: -1}
DS_INT = {}
for i, a in S_INT.items():
    for j, b in D_INT.items():
        DS_INT[i + j] = DS_INT.get(i + j, 0) + a * b
UX, UY, UZ = 0, 1, 2
OPACITY_GAIN = 5.0


def own_row(c, z, y):
    return (c * 4 + z) * 16 + y


PARTS = ((UX, True, 12), (UX, False, 8), (UY, True, 8), (UY, False, 8), (UZ, True, 12))


def message_rows():
    rows = []
    for c, inner, count in PARTS:
        for k in range(2):
            for i in range(count):
                rows.append((c, inner, k, i + (2 if count == 12 else 4)))
    return rows


def message_plane(inner, k, up):
    return (2 + k if inner else k) if up else (k if inner else 2 + k)


def send_matrix(up):
    w = np.zeros((96, 192), np.float32)
    for n, (c, inner, k, y) in enumerate(message_rows()):
        for dy, t in S_INT.items():
            w[n, own_row(c, message_plane(inner, k, up), y + dy)] += t
    return w


TERMS = (
    (0, UY, "S", "S", 1),
    (1, UZ, "S", "S", 1),
    (2, UZ, "S", "D", 1),
    (2, UY, "D", "S", -1),
    (3, UX, "S", "S", 1),
    (4, UX, "D", "S", 1),
    (5, UX, "S", "D", -1),
)
OWN_YZ, OWN_X, HALO_YZ, HALO_X = slice(64, 192), slice(0, 64), slice(32, 96), slice(0, 48)


def field_matrices():
    own = np.zeros((192, 192), np.float32)
    halo = {False: np.zeros((192, 96), np.float32), True: np.zeros((192, 96), np.float32)}
    place = {up: {} for up in (False, True)}
    for up in (False, True):
        for n, (c, inner, k, y) in enumerate(message_rows()):
            plane = message_plane(inner, k, up) + (-4 if up else 4)
            place[up][c, plane, y] = n
    along = {"S": S_INT, "D": DS_INT}
    for field, c, fz, fy, sign in TERMS:
        for p in range(4):
            for r in range(8):
                m = field * 32 + p * 8 + r
                for dz, a in along[fz].items():
                    q = p + dz
                    if 0 <= q < 4:
                        for dy, b in along[fy].items():
                            own[m, own_row(c, q, r + 4 + dy)] += sign * a * b
                    else:
                        up = q < 0
                        if fy == "S":
                            halo[up][m, place[up][c, q, r + 4]] += sign * a
                        else:
                            for dy, b in D_INT.items():
                                halo[up][m, place[up][c, q, r + 4 + dy]] += sign * a * b
    return own, halo[True], halo[False]


def line_matrix():
    w = np.zeros((256, 256), np.float32)
    for column, taps in ((0, S_INT), (128, DS_INT)):
        for j in range(128):
            for d, t in taps.items():
                row = j + d if 0 <= j + d < 128 else 128 + (j + d) % 128
                w[row, column + j] += t
    return w


def matrices():
    up, down = send_matrix(True), send_matrix(False)
    send = np.stack([np.concatenate([down, up]), np.concatenate([up, down])])
    own, prev, nxt = field_matrices()
    field = np.zeros((2, 192, 256), np.float32)
    for core, halo in enumerate(([prev, nxt], [nxt, prev])):
        field[core, :96] = np.concatenate([own[:96, OWN_YZ], *(h[:96, HALO_YZ] for h in halo)], 1)
        field[core, 96:, :160] = np.concatenate([own[96:, OWN_X], *(h[96:, HALO_X] for h in halo)], 1)
        assert not own[:96, OWN_X].any() and not own[96:, OWN_YZ].any()
        assert not any(h[:96, :32].any() or h[96:, 48:].any() for h in halo)
    return [m.astype(jnp.bfloat16) for m in (send, field, line_matrix())]


PAIRS = TILES // 2
TURN = 123
GROUP = 8
HBM = pl.BlockSpec(memory_space=pltpu.HBM)
VMEM = pl.BlockSpec(memory_space=pltpu.VMEM)


def in_hbm(x):
    return pltpu.with_memory_space_constraint(jnp.asarray(x), pltpu.HBM)


def core_index():
    return lax.rem(lax.axis_index("slab"), 2)


def pack_kernel(w_ref, f_ref, l_ref, x_ref, a_ref, b_ref, xv_ref, fv_ref, lv_ref, wv_ref, sems):
    core = core_index()
    parts = [slice(k * NX // 2, (k + 1) * NX // 2) for k in range(2)]
    sources = [w_ref.at[core]] + [x_ref.at[:, part] for part in parts] + [f_ref.at[core], l_ref]
    targets = [wv_ref] + [xv_ref.at[:, part] for part in parts] + [fv_ref, lv_ref]
    copies = [pltpu.make_async_copy(source, target, sems.at[n]) for n, (source, target) in enumerate(zip(sources, targets))]
    for copy in copies:
        copy.start()
    copies[0].wait()
    for copy, part in zip(copies[1:3], parts):
        copy.wait()
        out = jnp.dot(wv_ref[...], xv_ref[:, part], preferred_element_type=jnp.float32).astype(jnp.bfloat16)
        a_ref[:, part] = out[:96]
        b_ref[:, part] = out[96:]
    for copy in copies[3:]:
        copy.wait()


def pack(*arrays):
    out = [(96, NX), (96, NX), (192, NX), (192, 256), (256, 256)]
    return pl.pallas_call(
        pack_kernel,
        out_shape=[jax.ShapeDtypeStruct(shape, jnp.bfloat16) for shape in out],
        in_specs=[HBM] * 4,
        out_specs=[VMEM] * len(out),
        scratch_shapes=[pltpu.VMEM((192, 192), jnp.bfloat16), pltpu.SemaphoreType.DMA((5,))],
        compiler_params=pltpu.CompilerParams(vmem_limit_bytes=16 << 20),
        name="pack_halo",
    )(*arrays)


def line_image(l_ref, high_ref, low_ref, parity, out_ref):
    half = lax.broadcasted_iota(jnp.int32, (192, 128), 1) < 64

    def line(t):
        previous, here, following = (pl.ds((t + k) % TILES * 128, 128) for k in (-1, 0, 1))
        out = []
        for ref in (high_ref, low_ref):
            out += [ref[:, here], jnp.where(half, ref[:, following], ref[:, previous])]
        return jnp.concatenate(out, axis=1)

    def tile(yz, rest):
        smoothed = [rest[32:64], yz[:32, :128], yz[32:, :128]]
        curl = [rest[:32], rest[64:96] - yz[32:, 128:], rest[96:] + yz[:32, 128:]]
        density = (curl[0] * curl[0] + curl[1] * curl[1] + curl[2] * curl[2]) * (OPACITY_GAIN / 1024.0 / 49152.0**2)
        colours = [0.5 + 0.5 * jnp.tanh(s * (1.0 / 4096.0)) for s in smoothed]
        opacity = 1.0 - jnp.exp(-density)
        depth = density[:8]
        weight = opacity[:8]
        sums = [weight * c[:8] for c in colours]
        for p in range(1, 4):
            part = slice(8 * p, 8 * p + 8)
            weight = jnp.exp(-depth) * opacity[part]
            sums = [s + weight * c[part] for s, c in zip(sums, colours)]
            depth = depth + density[part]
        return sums + [depth]

    both = jnp.concatenate([l_ref[...]] * 2, axis=0)
    for first in range(0, PAIRS, GROUP):
        lines = [line(2 * (first + n) + parity) for n in range(GROUP)]
        yz = jnp.dot(jnp.concatenate([v[:64] for v in lines], axis=0), both, preferred_element_type=jnp.float32)
        rest = jnp.dot(jnp.concatenate([v[64:] for v in lines], axis=0), both[:, :128], preferred_element_type=jnp.float32)
        for n in range(GROUP):
            for f, value in enumerate(tile(yz[n * 64 : n * 64 + 64], rest[n * 128 : n * 128 + 128])):
                row = (f * PAIRS + first + n) * 8
                out_ref[row : row + 8, :] = value


def first_image_kernel(w_ref, l_ref, x_ref, a_ref, b_ref, send_ref, high_ref, low_ref):
    for n in range(0, NX, 256):
        cols = slice(n, n + 256)
        yz = jnp.concatenate([x_ref[OWN_YZ, cols], a_ref[HALO_YZ, cols], b_ref[HALO_YZ, cols]], axis=0)
        x = jnp.concatenate([x_ref[OWN_X, cols], a_ref[HALO_X, cols], b_ref[HALO_X, cols]], axis=0)
        out = jnp.concatenate(
            [
                jnp.dot(w_ref[:96, :], yz, preferred_element_type=jnp.float32),
                jnp.dot(w_ref[96:, :160], x, preferred_element_type=jnp.float32),
            ],
            axis=0,
        )
        high = out.astype(jnp.bfloat16)
        high_ref[:, cols] = high
        low_ref[:, cols] = (out - high.astype(jnp.float32)).astype(jnp.bfloat16)
    core = core_index()
    for parity in range(2):

        @pl.when(core == 1 - parity)
        def _(parity=parity):
            line_image(l_ref, high_ref, low_ref, parity, send_ref)


def second_image_kernel(l_ref, high_ref, low_ref, keep_ref):
    core = core_index()
    for parity in range(2):

        @pl.when(core == parity)
        def _(parity=parity):
            line_image(l_ref, high_ref, low_ref, parity, keep_ref)


def image_call(kernel, name, outs, *arrays):
    return pl.pallas_call(
        kernel,
        out_shape=outs,
        in_specs=[VMEM] * len(arrays),
        out_specs=[VMEM] * len(outs),
        compiler_params=pltpu.CompilerParams(vmem_limit_bytes=16 << 20),
        cost_estimate=pl.CostEstimate(flops=2 * 192 * 1024 * NX, bytes_accessed=1 << 20, transcendentals=0),
        name=name,
    )(*arrays)


def first_image(*arrays):
    image, field = jax.ShapeDtypeStruct((PAIRS * 32, 128), jnp.float32), jax.ShapeDtypeStruct((192, NX), jnp.bfloat16)
    return image_call(first_image_kernel, "send_image", [image, field, field], *arrays)


def second_image(*arrays):
    image = jax.ShapeDtypeStruct((PAIRS * 32, 128), jnp.float32)
    return image_call(second_image_kernel, "keep_image", [image], *arrays)[0]


def merge_kernel(own_ref, other_ref, out_ref):
    first = core_index() == 0
    own, other = ([ref[f * PAIRS * 8 : (f + 1) * PAIRS * 8, :] for f in range(4)] for ref in (own_ref, other_ref))
    zero = jnp.zeros_like(own[3])
    own_scale = jnp.exp(-jnp.where(first, zero, other[3]))
    other_scale = jnp.exp(-jnp.where(first, own[3], zero))
    merged = [own_scale * a + other_scale * b for a, b in zip(own[:3], other[:3])] + [own[3] + other[3]]
    for f in range(4):
        for pair in range(PAIRS):
            rank = (pair - TURN) % 128
            value, turn = merged[f][pair * 8 : pair * 8 + 8], rank // 16
            out_ref[pl.ds(rank % 16 * 4 + f, 8, stride=64), :] = pltpu.roll(value, turn, 0) if turn else value


def merge(own, other):
    return pl.pallas_call(
        merge_kernel,
        out_shape=jax.ShapeDtypeStruct((512, 128), jnp.float32),
        in_specs=[VMEM] * 2,
        out_specs=VMEM,
        compiler_params=pltpu.CompilerParams(vmem_limit_bytes=8 << 20),
        name="merge_cores",
    )(own, other)


def composite_kernel(in_ref, out_ref):
    lead = (-TURN) % 128 // 16

    def part(v, f):
        rank = (v - TURN) % 128
        value = in_ref[pl.ds(rank % 16 * 4 + f, 8, stride=64), :]
        turn = (lead - rank // 16) % 8
        return pltpu.roll(value, turn, 0) if turn else value

    depth = part(0, 3)
    sums = [part(0, f) for f in range(3)]
    for v in range(1, 16):
        through = jnp.exp(-depth)
        sums = [s + through * part(v, f) for f, s in enumerate(sums)]
        depth = depth + part(v, 3)
    nearer, total = {}, jnp.zeros((1, 128), jnp.float32)
    for segment in range(8):
        sublane = (segment + lead) % 8
        nearer[sublane] = total
        total = total + depth[sublane : sublane + 1]
    through = jnp.exp(-jnp.concatenate([nearer[s] for s in range(8)], axis=0))
    for f in range(3):
        out_ref[f : f + 1, :] = jnp.sum(through * sums[f], axis=0, keepdims=True)
    out_ref[3:4, :] = 1.0 - jnp.exp(-total)


def composite(parts):
    return pl.pallas_call(
        composite_kernel,
        out_shape=jax.ShapeDtypeStruct((4, 128), jnp.float32),
        in_specs=[VMEM],
        out_specs=VMEM,
        compiler_params=pltpu.CompilerParams(vmem_limit_bytes=8 << 20),
        name="composite_chips",
    )(parts)


def solution(mesh):
    devices = mesh.shape["slab"]
    weights = matrices()
    across = [(i, (i + 1) % devices if i % 2 else (i - 1) % devices) for i in range(devices)]
    within = [(i, i ^ 1) for i in range(devices)]
    same_core = [[(2 * (c + TURN) + k) % devices for c in range(devices // 2)] for k in range(2)]

    def per_device(velocity):
        x = in_hbm(velocity.reshape(192, NX))
        to_chip, to_core, x, field_w, line_w = pack(*map(in_hbm, weights), x)
        from_chip = lax.ppermute(to_chip, "slab", across)
        from_core = lax.ppermute(to_core, "slab", within)
        send, high, low = first_image(field_w, line_w, x, from_chip, from_core)
        other = lax.ppermute(send, "slab", within)
        keep = second_image(line_w, high, low)
        merged = merge(keep, other).reshape(128, 4, 128)
        gathered = lax.all_to_all(merged, "slab", 0, 0, axis_index_groups=same_core, tiled=True)
        return composite(gathered.reshape(512, 128))

    return jax.shard_map(per_device, mesh=mesh, in_specs=(P(None, "slab", None, None),), out_specs=P(None, "slab"), check_vma=False)
```

```python
import numpy as np
import jax
import jax.numpy as jnp
from jax import lax
from jax.experimental import pallas as pl
from jax.experimental.pallas import tpu as pltpu
from jax.sharding import PartitionSpec as P

NX = 4096
TILES = NX // 128
S_INT = {-2: 1, -1: 4, 0: 6, 1: 4, 2: 1}
D_INT = {-2: 1, -1: -8, 1: 8, 2: -1}
DS_INT = {}
for i, a in S_INT.items():
    for j, b in D_INT.items():
        DS_INT[i + j] = DS_INT.get(i + j, 0) + a * b
UX, UY, UZ = 0, 1, 2
OPACITY_GAIN = 5.0


def own_row(c, z, y):
    return (c * 4 + z) * 16 + y


PARTS = ((UX, True, 12), (UX, False, 8), (UY, True, 8), (UY, False, 8), (UZ, True, 12))


def message_rows():
    rows = []
    for c, inner, count in PARTS:
        for k in range(2):
            for i in range(count):
                rows.append((c, inner, k, i + (2 if count == 12 else 4)))
    return rows


def message_plane(inner, k, up):
    return (2 + k if inner else k) if up else (k if inner else 2 + k)


def send_matrix(up):
    w = np.zeros((96, 192), np.float32)
    for n, (c, inner, k, y) in enumerate(message_rows()):
        for dy, t in S_INT.items():
            w[n, own_row(c, message_plane(inner, k, up), y + dy)] += t
    return w


TERMS = (
    (0, UY, "S", "S", 1),
    (1, UZ, "S", "S", 1),
    (2, UZ, "S", "D", 1),
    (2, UY, "D", "S", -1),
    (3, UX, "S", "S", 1),
    (4, UX, "D", "S", 1),
    (5, UX, "S", "D", -1),
)
OWN_YZ, OWN_X, HALO_YZ, HALO_X = slice(64, 192), slice(0, 64), slice(32, 96), slice(0, 48)


def field_matrices():
    own = np.zeros((192, 192), np.float32)
    halo = {False: np.zeros((192, 96), np.float32), True: np.zeros((192, 96), np.float32)}
    place = {up: {} for up in (False, True)}
    for up in (False, True):
        for n, (c, inner, k, y) in enumerate(message_rows()):
            plane = message_plane(inner, k, up) + (-4 if up else 4)
            place[up][c, plane, y] = n
    along = {"S": S_INT, "D": DS_INT}
    for field, c, fz, fy, sign in TERMS:
        for p in range(4):
            for r in range(8):
                m = field * 32 + p * 8 + r
                for dz, a in along[fz].items():
                    q = p + dz
                    if 0 <= q < 4:
                        for dy, b in along[fy].items():
                            own[m, own_row(c, q, r + 4 + dy)] += sign * a * b
                    else:
                        up = q < 0
                        if fy == "S":
                            halo[up][m, place[up][c, q, r + 4]] += sign * a
                        else:
                            for dy, b in D_INT.items():
                                halo[up][m, place[up][c, q, r + 4 + dy]] += sign * a * b
    return own, halo[True], halo[False]


def line_matrix():
    w = np.zeros((256, 256), np.float32)
    for column, taps in ((0, S_INT), (128, DS_INT)):
        for j in range(128):
            for d, t in taps.items():
                row = j + d if 0 <= j + d < 128 else 128 + (j + d) % 128
                w[row, column + j] += t
    return w


def matrices():
    up, down = send_matrix(True), send_matrix(False)
    send = np.stack([np.concatenate([down, up]), np.concatenate([up, down])])
    own, prev, nxt = field_matrices()
    field = np.zeros((2, 192, 256), np.float32)
    for core, halo in enumerate(([prev, nxt], [nxt, prev])):
        field[core, :96] = np.concatenate([own[:96, OWN_YZ], *(h[:96, HALO_YZ] for h in halo)], 1)
        field[core, 96:, :160] = np.concatenate([own[96:, OWN_X], *(h[96:, HALO_X] for h in halo)], 1)
        assert not own[:96, OWN_X].any() and not own[96:, OWN_YZ].any()
        assert not any(h[:96, :32].any() or h[96:, 48:].any() for h in halo)
    return [m.astype(jnp.bfloat16) for m in (send, field, line_matrix())]


PAIRS = TILES // 2
TURN = 122
GROUP = 8
HBM = pl.BlockSpec(memory_space=pltpu.HBM)
VMEM = pl.BlockSpec(memory_space=pltpu.VMEM)


def in_hbm(x):
    return pltpu.with_memory_space_constraint(jnp.asarray(x), pltpu.HBM)


def core_index():
    return lax.rem(lax.axis_index("slab"), 2)


def pack_kernel(w_ref, f_ref, l_ref, x_ref, a_ref, xv_ref, wv_ref, fv_ref, lv_ref, sems):
    core = core_index()
    parts = [slice(k * NX // 2, (k + 1) * NX // 2) for k in range(2)]
    sources = [w_ref.at[core]] + [x_ref.at[:, part] for part in parts] + [f_ref.at[core], l_ref]
    targets = [wv_ref] + [xv_ref.at[:, part] for part in parts] + [fv_ref, lv_ref]
    copies = [pltpu.make_async_copy(source, target, sems.at[n]) for n, (source, target) in enumerate(zip(sources, targets))]
    for copy in copies:
        copy.start()
    copies[0].wait()
    for copy, part in zip(copies[1:3], parts):
        copy.wait()
        a_ref[:, part] = jnp.dot(wv_ref[:96, :], xv_ref[:, part], preferred_element_type=jnp.float32).astype(jnp.bfloat16)
    for copy in copies[3:]:
        copy.wait()


def pack(*arrays):
    out = [(96, NX), (192, NX), (192, 192), (192, 256), (256, 256)]
    return pl.pallas_call(
        pack_kernel,
        out_shape=[jax.ShapeDtypeStruct(shape, jnp.bfloat16) for shape in out],
        in_specs=[HBM] * 4,
        out_specs=[VMEM] * len(out),
        scratch_shapes=[pltpu.SemaphoreType.DMA((5,))],
        compiler_params=pltpu.CompilerParams(vmem_limit_bytes=16 << 20),
        name="pack_halo",
    )(*arrays)


def pack_core_kernel(w_ref, x_ref, *b_refs):
    for part, b_ref in zip((slice(0, NX // 2), slice(NX // 2, NX)), b_refs):
        b_ref[...] = jnp.dot(w_ref[96:, :], x_ref[:, part], preferred_element_type=jnp.float32).astype(jnp.bfloat16)


def pack_core(*arrays):
    return image_call(pack_core_kernel, "pack_core", [jax.ShapeDtypeStruct((96, NX // 2), jnp.bfloat16)] * 2, *arrays)


def line_image(l_ref, high_ref, low_ref, parity, out_ref):
    half = lax.broadcasted_iota(jnp.int32, (192, 128), 1) < 64

    def line(t):
        previous, here, following = (pl.ds((t + k) % TILES * 128, 128) for k in (-1, 0, 1))
        out = []
        for ref in (high_ref, low_ref):
            out += [ref[:, here], jnp.where(half, ref[:, following], ref[:, previous])]
        return jnp.concatenate(out, axis=1)

    def tile(yz, rest):
        smoothed = [rest[32:64], yz[:32, :128], yz[32:, :128]]
        curl = [rest[:32], rest[64:96] - yz[32:, 128:], rest[96:] + yz[:32, 128:]]
        density = (curl[0] * curl[0] + curl[1] * curl[1] + curl[2] * curl[2]) * (OPACITY_GAIN / 1024.0 / 49152.0**2)
        colours = [0.5 + 0.5 * jnp.tanh(s * (1.0 / 4096.0)) for s in smoothed]
        opacity = 1.0 - jnp.exp(-density)
        depth = density[:8]
        weight = opacity[:8]
        sums = [weight * c[:8] for c in colours]
        for p in range(1, 4):
            part = slice(8 * p, 8 * p + 8)
            weight = jnp.exp(-depth) * opacity[part]
            sums = [s + weight * c[part] for s, c in zip(sums, colours)]
            depth = depth + density[part]
        return sums + [depth]

    both = jnp.concatenate([l_ref[...]] * 2, axis=0)
    for first in range(0, PAIRS, GROUP):
        lines = [line(2 * (first + n) + parity) for n in range(GROUP)]
        yz = jnp.dot(jnp.concatenate([v[:64] for v in lines], axis=0), both, preferred_element_type=jnp.float32)
        rest = jnp.dot(jnp.concatenate([v[64:] for v in lines], axis=0), both[:, :128], preferred_element_type=jnp.float32)
        for n in range(GROUP):
            for f, value in enumerate(tile(yz[n * 64 : n * 64 + 64], rest[n * 128 : n * 128 + 128])):
                row = (f * PAIRS + first + n) * 8
                out_ref[row : row + 8, :] = value


def zy_fields(w_ref, x_ref, a_ref, b_ref, high_ref, low_ref, cols):
    half = slice(cols.start % (NX // 2), cols.start % (NX // 2) + cols.stop - cols.start)
    yz = jnp.concatenate([x_ref[OWN_YZ, cols], a_ref[HALO_YZ, cols], b_ref[HALO_YZ, half]], axis=0)
    x = jnp.concatenate([x_ref[OWN_X, cols], a_ref[HALO_X, cols], b_ref[HALO_X, half]], axis=0)
    out = jnp.concatenate(
        [
            jnp.dot(w_ref[:96, :], yz, preferred_element_type=jnp.float32),
            jnp.dot(w_ref[96:, :160], x, preferred_element_type=jnp.float32),
        ],
        axis=0,
    )
    high = out.astype(jnp.bfloat16)
    high_ref[:, cols] = high
    low_ref[:, cols] = (out - high.astype(jnp.float32)).astype(jnp.bfloat16)


def first_image_kernel(w_ref, l_ref, x_ref, a_ref, b0_ref, b1_ref, send_ref, high_ref, low_ref):
    core = core_index()
    for parity in range(2):

        @pl.when(core == 1 - parity)
        def _(parity=parity):
            for n in range(0, NX, 512):
                zy_fields(w_ref, x_ref, a_ref, (b0_ref, b1_ref)[n // (NX // 2)], high_ref, low_ref, slice(n, n + 512))
            line_image(l_ref, high_ref, low_ref, parity, send_ref)


def second_image_kernel(l_ref, high_ref, low_ref, keep_ref):
    core = core_index()
    for parity in range(2):

        @pl.when(core == parity)
        def _(parity=parity):
            line_image(l_ref, high_ref, low_ref, parity, keep_ref)


def image_call(kernel, name, outs, *arrays):
    return pl.pallas_call(
        kernel,
        out_shape=outs,
        in_specs=[VMEM] * len(arrays),
        out_specs=[VMEM] * len(outs),
        compiler_params=pltpu.CompilerParams(vmem_limit_bytes=16 << 20),
        cost_estimate=pl.CostEstimate(flops=2 * 192 * 1024 * NX, bytes_accessed=1 << 20, transcendentals=0),
        name=name,
    )(*arrays)


def first_image(*arrays):
    image, field = jax.ShapeDtypeStruct((PAIRS * 32, 128), jnp.float32), jax.ShapeDtypeStruct((192, NX), jnp.bfloat16)
    return image_call(first_image_kernel, "send_image", [image, field, field], *arrays)


def second_image(*arrays):
    image = jax.ShapeDtypeStruct((PAIRS * 32, 128), jnp.float32)
    return image_call(second_image_kernel, "keep_image", [image], *arrays)[0]


def merge_kernel(own_ref, other_ref, out_ref):
    first = core_index() == 0
    own, other = ([ref[f * PAIRS * 8 : (f + 1) * PAIRS * 8, :] for f in range(4)] for ref in (own_ref, other_ref))
    zero = jnp.zeros_like(own[3])
    own_scale = jnp.exp(-jnp.where(first, zero, other[3]))
    other_scale = jnp.exp(-jnp.where(first, own[3], zero))
    merged = [own_scale * a + other_scale * b for a, b in zip(own[:3], other[:3])] + [own[3] + other[3]]
    for f in range(4):
        for pair in range(PAIRS):
            rank = (pair - TURN) % 128
            value, turn = merged[f][pair * 8 : pair * 8 + 8], rank // 16
            out_ref[pl.ds(rank % 16 * 4 + f, 8, stride=64), :] = pltpu.roll(value, turn, 0) if turn else value


def merge(own, other):
    return pl.pallas_call(
        merge_kernel,
        out_shape=jax.ShapeDtypeStruct((512, 128), jnp.float32),
        in_specs=[VMEM] * 2,
        out_specs=VMEM,
        compiler_params=pltpu.CompilerParams(vmem_limit_bytes=8 << 20),
        name="merge_cores",
    )(own, other)


def composite_kernel(in_ref, out_ref):
    lead = (-TURN) % 128 // 16

    def part(v, f):
        rank = (v - TURN) % 128
        value = in_ref[pl.ds(rank % 16 * 4 + f, 8, stride=64), :]
        turn = (lead - rank // 16) % 8
        return pltpu.roll(value, turn, 0) if turn else value

    depth = part(0, 3)
    sums = [part(0, f) for f in range(3)]
    for v in range(1, 16):
        through = jnp.exp(-depth)
        sums = [s + through * part(v, f) for f, s in enumerate(sums)]
        depth = depth + part(v, 3)
    nearer, total = {}, jnp.zeros((1, 128), jnp.float32)
    for segment in range(8):
        sublane = (segment + lead) % 8
        nearer[sublane] = total
        total = total + depth[sublane : sublane + 1]
    through = jnp.exp(-jnp.concatenate([nearer[s] for s in range(8)], axis=0))
    for f in range(3):
        out_ref[f : f + 1, :] = jnp.sum(through * sums[f], axis=0, keepdims=True)
    out_ref[3:4, :] = 1.0 - jnp.exp(-total)


def composite(parts):
    return pl.pallas_call(
        composite_kernel,
        out_shape=jax.ShapeDtypeStruct((4, 128), jnp.float32),
        in_specs=[VMEM],
        out_specs=VMEM,
        compiler_params=pltpu.CompilerParams(vmem_limit_bytes=8 << 20),
        name="composite_chips",
    )(parts)


def solution(mesh):
    devices = mesh.shape["slab"]
    weights = matrices()
    across = [(i, (i + 1) % devices if i % 2 else (i - 1) % devices) for i in range(devices)]
    within = [(i, i ^ 1) for i in range(devices)]
    same_core = [[(2 * (c + TURN) + k) % devices for c in range(devices // 2)] for k in range(2)]

    def per_device(velocity):
        x = in_hbm(velocity.reshape(192, NX))
        to_chip, x, send_w, field_w, line_w = pack(*map(in_hbm, weights), x)
        from_chip = lax.ppermute(to_chip, "slab", across)
        from_core = [lax.ppermute(part, "slab", within) for part in pack_core(send_w, x)]
        send, high, low = first_image(field_w, line_w, x, from_chip, *from_core)
        other = lax.ppermute(send, "slab", within)
        keep = second_image(line_w, high, low)
        merged = merge(keep, other).reshape(128, 4, 128)
        gathered = lax.all_to_all(merged, "slab", 0, 0, axis_index_groups=same_core, tiled=True)
        return composite(gathered.reshape(512, 128))

    return jax.shard_map(per_device, mesh=mesh, in_specs=(P(None, "slab", None, None),), out_specs=P(None, "slab"), check_vma=False)
```

```python
import numpy as np
import jax
import jax.numpy as jnp
from jax import lax
from jax.experimental import pallas as pl
from jax.experimental.pallas import tpu as pltpu
from jax.sharding import PartitionSpec as P

NX = 4096
TILES = NX // 128
S_INT = {-2: 1, -1: 4, 0: 6, 1: 4, 2: 1}
D_INT = {-2: 1, -1: -8, 1: 8, 2: -1}
DS_INT = {}
for i, a in S_INT.items():
    for j, b in D_INT.items():
        DS_INT[i + j] = DS_INT.get(i + j, 0) + a * b
UX, UY, UZ = 0, 1, 2
OPACITY_GAIN = 5.0


def own_row(c, z, y):
    return (c * 4 + z) * 16 + y


PARTS = ((UX, True, 12), (UX, False, 8), (UY, True, 8), (UY, False, 8), (UZ, True, 12))


def message_rows():
    rows = []
    for c, inner, count in PARTS:
        for k in range(2):
            for i in range(count):
                rows.append((c, inner, k, i + (2 if count == 12 else 4)))
    return rows


def message_plane(inner, k, up):
    return (2 + k if inner else k) if up else (k if inner else 2 + k)


def send_matrix(up):
    w = np.zeros((96, 192), np.float32)
    for n, (c, inner, k, y) in enumerate(message_rows()):
        for dy, t in S_INT.items():
            w[n, own_row(c, message_plane(inner, k, up), y + dy)] += t
    return w


TERMS = (
    (0, UY, "S", "S", 1),
    (1, UZ, "S", "S", 1),
    (2, UZ, "S", "D", 1),
    (2, UY, "D", "S", -1),
    (3, UX, "S", "S", 1),
    (4, UX, "D", "S", 1),
    (5, UX, "S", "D", -1),
)
OWN_YZ, OWN_X, HALO_YZ, HALO_X = slice(64, 192), slice(0, 64), slice(32, 96), slice(0, 48)


def field_matrices():
    own = np.zeros((192, 192), np.float32)
    halo = {False: np.zeros((192, 96), np.float32), True: np.zeros((192, 96), np.float32)}
    place = {up: {} for up in (False, True)}
    for up in (False, True):
        for n, (c, inner, k, y) in enumerate(message_rows()):
            plane = message_plane(inner, k, up) + (-4 if up else 4)
            place[up][c, plane, y] = n
    along = {"S": S_INT, "D": DS_INT}
    for field, c, fz, fy, sign in TERMS:
        for p in range(4):
            for r in range(8):
                m = field * 32 + p * 8 + r
                for dz, a in along[fz].items():
                    q = p + dz
                    if 0 <= q < 4:
                        for dy, b in along[fy].items():
                            own[m, own_row(c, q, r + 4 + dy)] += sign * a * b
                    else:
                        up = q < 0
                        if fy == "S":
                            halo[up][m, place[up][c, q, r + 4]] += sign * a
                        else:
                            for dy, b in D_INT.items():
                                halo[up][m, place[up][c, q, r + 4 + dy]] += sign * a * b
    return own, halo[True], halo[False]


def line_matrix():
    w = np.zeros((256, 256), np.float32)
    for column, taps in ((0, S_INT), (128, DS_INT)):
        for j in range(128):
            for d, t in taps.items():
                row = j + d if 0 <= j + d < 128 else 128 + (j + d) % 128
                w[row, column + j] += t
    return w


def matrices():
    up, down = send_matrix(True), send_matrix(False)
    send = np.stack([np.concatenate([down, up]), np.concatenate([up, down])])
    own, prev, nxt = field_matrices()
    field = np.zeros((2, 192, 384), np.float32)
    for core, (across, within) in enumerate(((prev, nxt), (nxt, prev))):
        field[core, :96, :192] = np.concatenate([own[:96, OWN_YZ], within[:96, HALO_YZ]], 1)
        field[core, 96:, :112] = np.concatenate([own[96:, OWN_X], within[96:, HALO_X]], 1)
        field[core, :, 256:352] = across
        assert not own[:96, OWN_X].any() and not own[96:, OWN_YZ].any()
        assert not within[:96, :32].any() and not within[96:, 48:].any()
    return [m.astype(jnp.bfloat16) for m in (send, field, line_matrix())]


PAIRS = TILES // 2
TURN = 126
GROUP = 8
HBM = pl.BlockSpec(memory_space=pltpu.HBM)
VMEM = pl.BlockSpec(memory_space=pltpu.VMEM)


def in_hbm(x):
    return pltpu.with_memory_space_constraint(jnp.asarray(x), pltpu.HBM)


def core_index():
    return lax.rem(lax.axis_index("slab"), 2)


def pack_kernel(w_ref, f_ref, l_ref, x_ref, a_ref, xv_ref, wv_ref, fv_ref, lv_ref, sems):
    core = core_index()
    parts = [slice(k * NX // 2, (k + 1) * NX // 2) for k in range(2)]
    sources = [w_ref.at[core]] + [x_ref.at[:, part] for part in parts] + [f_ref.at[core], l_ref]
    targets = [wv_ref] + [xv_ref.at[:, part] for part in parts] + [fv_ref, lv_ref]
    copies = [pltpu.make_async_copy(source, target, sems.at[n]) for n, (source, target) in enumerate(zip(sources, targets))]
    for copy in copies:
        copy.start()
    copies[0].wait()
    for copy, part in zip(copies[1:3], parts):
        copy.wait()
        a_ref[:, part] = jnp.dot(wv_ref[:96, :], xv_ref[:, part], preferred_element_type=jnp.float32).astype(jnp.bfloat16)
    for copy in copies[3:]:
        copy.wait()


def pack(*arrays):
    out = [(96, NX), (192, NX), (192, 192), (192, 384), (256, 256)]
    return pl.pallas_call(
        pack_kernel,
        out_shape=[jax.ShapeDtypeStruct(shape, jnp.bfloat16) for shape in out],
        in_specs=[HBM] * 4,
        out_specs=[VMEM] * len(out),
        scratch_shapes=[pltpu.SemaphoreType.DMA((5,))],
        compiler_params=pltpu.CompilerParams(vmem_limit_bytes=16 << 20),
        name="pack_halo",
    )(*arrays)


def pack_core_kernel(w_ref, x_ref, *b_refs):
    for part, b_ref in zip((slice(0, NX // 2), slice(NX // 2, NX)), b_refs):
        b_ref[...] = jnp.dot(w_ref[96:, :], x_ref[:, part], preferred_element_type=jnp.float32).astype(jnp.bfloat16)


def pack_core(*arrays):
    return image_call(pack_core_kernel, "pack_core", [jax.ShapeDtypeStruct((96, NX // 2), jnp.bfloat16)] * 2, *arrays)


def line_image(l_ref, high_ref, low_ref, parity, out_ref):
    half = lax.broadcasted_iota(jnp.int32, (192, 128), 1) < 64

    def line(t):
        previous, here, following = (pl.ds((t + k) % TILES * 128, 128) for k in (-1, 0, 1))
        out = []
        for ref in (high_ref, low_ref):
            out += [ref[:, here], jnp.where(half, ref[:, following], ref[:, previous])]
        return jnp.concatenate(out, axis=1)

    def tile(yz, rest):
        smoothed = [rest[32:64], yz[:32, :128], yz[32:, :128]]
        curl = [rest[:32], rest[64:96] - yz[32:, 128:], rest[96:] + yz[:32, 128:]]
        density = (curl[0] * curl[0] + curl[1] * curl[1] + curl[2] * curl[2]) * (OPACITY_GAIN / 1024.0 / 49152.0**2)
        colours = [0.5 + 0.5 * jnp.tanh(s * (1.0 / 4096.0)) for s in smoothed]
        opacity = 1.0 - jnp.exp(-density)
        depth = density[:8]
        weight = opacity[:8]
        sums = [weight * c[:8] for c in colours]
        for p in range(1, 4):
            part = slice(8 * p, 8 * p + 8)
            weight = jnp.exp(-depth) * opacity[part]
            sums = [s + weight * c[part] for s, c in zip(sums, colours)]
            depth = depth + density[part]
        return sums + [depth]

    both = jnp.concatenate([l_ref[...]] * 2, axis=0)
    for first in range(0, PAIRS, GROUP):
        lines = [line(2 * (first + n) + parity) for n in range(GROUP)]
        yz = jnp.dot(jnp.concatenate([v[:64] for v in lines], axis=0), both, preferred_element_type=jnp.float32)
        rest = jnp.dot(jnp.concatenate([v[64:] for v in lines], axis=0), both[:, :128], preferred_element_type=jnp.float32)
        for n in range(GROUP):
            for f, value in enumerate(tile(yz[n * 64 : n * 64 + 64], rest[n * 128 : n * 128 + 128])):
                row = (f * PAIRS + first + n) * 8
                out_ref[row : row + 8, :] = value


def own_fields_kernel(w_ref, x_ref, b0_ref, b1_ref, part_ref):
    for n in range(0, NX, 512):
        cols, b_ref = slice(n, n + 512), (b0_ref, b1_ref)[n // (NX // 2)]
        half = slice(n % (NX // 2), n % (NX // 2) + 512)
        yz = jnp.concatenate([x_ref[OWN_YZ, cols], b_ref[HALO_YZ, half]], axis=0)
        x = jnp.concatenate([x_ref[OWN_X, cols], b_ref[HALO_X, half]], axis=0)
        part_ref[:96, cols] = jnp.dot(w_ref[:96, :192], yz, preferred_element_type=jnp.float32)
        part_ref[96:, cols] = jnp.dot(w_ref[96:, :112], x, preferred_element_type=jnp.float32)


def own_fields(*arrays):
    return image_call(own_fields_kernel, "own_fields", [jax.ShapeDtypeStruct((192, NX), jnp.float32)], *arrays)[0]


def first_image_kernel(w_ref, l_ref, part_ref, a_ref, send_ref, high_ref, low_ref):
    core = core_index()
    for parity in range(2):

        @pl.when(core == 1 - parity)
        def _(parity=parity):
            for n in range(0, NX, 512):
                cols = slice(n, n + 512)
                out = part_ref[:, cols] + jnp.dot(w_ref[:, 256:352], a_ref[:, cols], preferred_element_type=jnp.float32)
                high = out.astype(jnp.bfloat16)
                high_ref[:, cols] = high
                low_ref[:, cols] = (out - high.astype(jnp.float32)).astype(jnp.bfloat16)
            line_image(l_ref, high_ref, low_ref, parity, send_ref)


def second_image_kernel(l_ref, high_ref, low_ref, keep_ref):
    core = core_index()
    for parity in range(2):

        @pl.when(core == parity)
        def _(parity=parity):
            line_image(l_ref, high_ref, low_ref, parity, keep_ref)


def image_call(kernel, name, outs, *arrays):
    return pl.pallas_call(
        kernel,
        out_shape=outs,
        in_specs=[VMEM] * len(arrays),
        out_specs=[VMEM] * len(outs),
        compiler_params=pltpu.CompilerParams(vmem_limit_bytes=16 << 20),
        cost_estimate=pl.CostEstimate(flops=2 * 192 * 1024 * NX, bytes_accessed=1 << 20, transcendentals=0),
        name=name,
    )(*arrays)


def first_image(*arrays):
    image, field = jax.ShapeDtypeStruct((PAIRS * 32, 128), jnp.float32), jax.ShapeDtypeStruct((192, NX), jnp.bfloat16)
    return image_call(first_image_kernel, "send_image", [image, field, field], *arrays)


def second_image(*arrays):
    image = jax.ShapeDtypeStruct((PAIRS * 32, 128), jnp.float32)
    return image_call(second_image_kernel, "keep_image", [image], *arrays)[0]


def merge_kernel(own_ref, other_ref, out_ref):
    first = core_index() == 0
    own, other = ([ref[f * PAIRS * 8 : (f + 1) * PAIRS * 8, :] for f in range(4)] for ref in (own_ref, other_ref))
    zero = jnp.zeros_like(own[3])
    own_scale = jnp.exp(-jnp.where(first, zero, other[3]))
    other_scale = jnp.exp(-jnp.where(first, own[3], zero))
    merged = [own_scale * a + other_scale * b for a, b in zip(own[:3], other[:3])] + [own[3] + other[3]]
    for f in range(4):
        for pair in range(PAIRS):
            rank = (pair - TURN) % 128
            value, turn = merged[f][pair * 8 : pair * 8 + 8], rank // 16
            out_ref[pl.ds(rank % 16 * 4 + f, 8, stride=64), :] = pltpu.roll(value, turn, 0) if turn else value


def merge(own, other):
    return pl.pallas_call(
        merge_kernel,
        out_shape=jax.ShapeDtypeStruct((512, 128), jnp.float32),
        in_specs=[VMEM] * 2,
        out_specs=VMEM,
        compiler_params=pltpu.CompilerParams(vmem_limit_bytes=8 << 20),
        name="merge_cores",
    )(own, other)


def composite_kernel(in_ref, out_ref):
    lead = (-TURN) % 128 // 16

    def part(v, f):
        rank = (v - TURN) % 128
        value = in_ref[pl.ds(rank % 16 * 4 + f, 8, stride=64), :]
        turn = (lead - rank // 16) % 8
        return pltpu.roll(value, turn, 0) if turn else value

    depth = part(0, 3)
    sums = [part(0, f) for f in range(3)]
    for v in range(1, 16):
        through = jnp.exp(-depth)
        sums = [s + through * part(v, f) for f, s in enumerate(sums)]
        depth = depth + part(v, 3)
    nearer, total = {}, jnp.zeros((1, 128), jnp.float32)
    for segment in range(8):
        sublane = (segment + lead) % 8
        nearer[sublane] = total
        total = total + depth[sublane : sublane + 1]
    through = jnp.exp(-jnp.concatenate([nearer[s] for s in range(8)], axis=0))
    for f in range(3):
        out_ref[f : f + 1, :] = jnp.sum(through * sums[f], axis=0, keepdims=True)
    out_ref[3:4, :] = 1.0 - jnp.exp(-total)


def composite(parts):
    return pl.pallas_call(
        composite_kernel,
        out_shape=jax.ShapeDtypeStruct((4, 128), jnp.float32),
        in_specs=[VMEM],
        out_specs=VMEM,
        compiler_params=pltpu.CompilerParams(vmem_limit_bytes=8 << 20),
        name="composite_chips",
    )(parts)


def solution(mesh):
    devices = mesh.shape["slab"]
    weights = matrices()
    across = [(i, (i + 1) % devices if i % 2 else (i - 1) % devices) for i in range(devices)]
    within = [(i, i ^ 1) for i in range(devices)]
    same_core = [[(2 * (c + TURN) + k) % devices for c in range(devices // 2)] for k in range(2)]

    def per_device(velocity):
        x = in_hbm(velocity.reshape(192, NX))
        to_chip, x, send_w, field_w, line_w = pack(*map(in_hbm, weights), x)
        from_chip = lax.ppermute(to_chip, "slab", across)
        from_core = [lax.ppermute(part, "slab", within) for part in pack_core(send_w, x)]
        part = own_fields(field_w, x, *from_core)
        send, high, low = first_image(field_w, line_w, part, from_chip)
        other = lax.ppermute(send, "slab", within)
        keep = second_image(line_w, high, low)
        merged = merge(keep, other).reshape(128, 4, 128)
        gathered = lax.all_to_all(merged, "slab", 0, 0, axis_index_groups=same_core, tiled=True)
        return composite(gathered.reshape(512, 128))

    return jax.shard_map(per_device, mesh=mesh, in_specs=(P(None, "slab", None, None),), out_specs=P(None, "slab"), check_vma=False)
```
